256 devices in a mesh: chan: 8 (over y, core), bl: 32 (over x, z).
Axes of the slice: x: 4, y: 4, z: 8, core: 2. Of those that a mesh axis runs over, the one named last changes fastest.
Arguments:
- visibility: float32 [8, 64, 2, 131072], P(None, 'chan', None, 'bl')
- model_vis: float32 [8, 64, 2, 131072], P(None, 'chan', None, 'bl')
- station_pairs: int32 [2, 131072], P(None, 'bl'), may hold values from 0 to 511, as said below
- init_gains: float32 [8, 64, 512], P(None, 'chan'), may hold values from -4 to 4
Outputs:
- solved_gains: float32 [8, 64, 512], P(None, 'chan')
The draws below stay inside these ranges and needn't reach their ends.
Inputs may be any that keep to these rules, and one draw needn't show every extreme that they name: `station_pairs`: each baseline joins two different stations; some baseline joins station 0 and station 512 - 1.
All inputs are finite; a program needn't handle non-finite values.
Results may differ from the reference program's by a relative error of at most 0.0001.
Values sent between devices are 32-bit elements; how exact they have to be, the bound alone decides.
A program may use at most 64 MiB of HBM per device.

```python
import jax
import jax.numpy as jnp
from jax import lax

NS = 512
NT = 2
ITERS = 3
NC = 64
NB = 131072


def jones_product_drawn(p, q):
    real = p[0][:, 0:1] * q[0][0:1] + p[0][:, 1:2] * q[0][1:2] - p[1][:, 0:1] * q[1][0:1] - p[1][:, 1:2] * q[1][1:2]
    imag = p[0][:, 0:1] * q[1][0:1] + p[0][:, 1:2] * q[1][1:2] + p[1][:, 0:1] * q[0][0:1] + p[1][:, 1:2] * q[0][1:2]
    return jnp.stack([real, imag])


def adjoint_drawn(p):
    return jnp.stack([jnp.swapaxes(p[0], 0, 1), -jnp.swapaxes(p[1], 0, 1)])


def pair_table(key):
    key_first, key_offset = jax.random.split(jax.random.fold_in(key, 11))
    first = jax.random.randint(key_first, (NB,), 0, NS)
    offset = jax.random.randint(key_offset, (NB,), 1, NS)
    second = (first + offset) % NS
    first = first.at[0].set(0)
    second = second.at[0].set(NS - 1)
    return (first, second)


def model_table(key):
    key_base = jax.random.fold_in(jax.random.fold_in(key, 23), 0)
    base = jax.random.normal(key_base, (8, NC, NT, NB), jnp.float32)
    return base


def true_gains(key):
    noise = 0.4 * jax.random.normal(jax.random.fold_in(key, 37), (2, 2, 2, NC, NS), jnp.float32)
    return noise.at[0, 0, 0].add(1.0).at[0, 1, 1].add(1.0)


def draw_station_pairs(key, part):
    first, second = pair_table(key)
    return jnp.stack([first, second]).astype(jnp.int32)


def draw_model_vis(key, part):
    return model_table(key)


def draw_visibility(key, part):
    first, second = pair_table(key)
    model = model_table(key).reshape(2, 2, 2, NC, NT, NB)
    gains = true_gains(key)
    gain_first = jnp.take(gains, first, axis=4)[:, :, :, :, None, :]
    gain_second = jnp.take(gains, second, axis=4)[:, :, :, :, None, :]
    clean = jones_product_drawn(jones_product_drawn(gain_first, model), adjoint_drawn(gain_second))
    noise = 0.3 * jax.random.normal(jax.random.fold_in(key, 41), (8, NC, NT, NB), jnp.float32)
    return clean.reshape(8, NC, NT, NB) + noise


def block_scale(key, dims, cuts, low, top_value):
    def one(dim, blocks):
        steps = jax.random.uniform(jax.random.fold_in(jax.random.fold_in(key, 6), dim), (blocks,), jnp.float32, low / len(cuts), top_value / len(cuts))
        return jnp.repeat(jnp.exp(steps), dims[dim] // blocks).reshape((-1,) + (1,) * (len(dims) - dim - 1))

    factor_of = one(*cuts[0])
    for cut in cuts[1:]:
        factor_of = factor_of * one(*cut)
    return factor_of


def centred(stream_key, dims, scale, reach, pieces=(), held_as=jnp.bfloat16):
    values = scale * jax.random.normal(stream_key, dims, jnp.float32)
    if pieces:
        values = values * block_scale(stream_key, dims, pieces, -0.22, 0.18)
    return jnp.clip(values, -reach, reach).astype(held_as)


def setup_inputs(seed: int = 0) -> dict:
    seeds = jax.random.split(jax.random.key(seed), 5)
    visibility = draw_visibility(jax.random.fold_in(seeds[4], 71), 0)
    model_vis = draw_model_vis(jax.random.fold_in(seeds[4], 71), 0)
    station_pairs = draw_station_pairs(jax.random.fold_in(seeds[4], 71), 0)
    init_gains = centred(seeds[3], (8, NC, NS), 0.5, 4.0, ((1, 8),), jnp.float32)
    return {"visibility": visibility, "model_vis": model_vis, "station_pairs": station_pairs, "init_gains": init_gains}


RIDGE = 1.0


def jones_product(p, q):
    real = p[0][:, 0:1] * q[0][0:1] + p[0][:, 1:2] * q[0][1:2] - p[1][:, 0:1] * q[1][0:1] - p[1][:, 1:2] * q[1][1:2]
    imag = p[0][:, 0:1] * q[1][0:1] + p[0][:, 1:2] * q[1][1:2] + p[1][:, 0:1] * q[0][0:1] + p[1][:, 1:2] * q[0][1:2]
    return jnp.stack([real, imag])


def adjoint(p):
    return jnp.stack([jnp.swapaxes(p[0], 0, 1), -jnp.swapaxes(p[1], 0, 1)])


def station_terms(vis, model, jones, first, second, stat_count):
    chan_count = vis.shape[3]
    base_count = vis.shape[5]
    gain_first = jnp.take(jones, first, axis=4)[:, :, :, :, None, :]
    gain_second = jnp.take(jones, second, axis=4)[:, :, :, :, None, :]
    ahead = jones_product(model, adjoint(gain_second))
    behind = jones_product(adjoint(model), adjoint(gain_first))
    numer_first = jnp.sum(jones_product(vis, adjoint(ahead)), axis=4)
    denom_first = jnp.sum(jones_product(ahead, adjoint(ahead)), axis=4)
    numer_second = jnp.sum(jones_product(adjoint(vis), adjoint(behind)), axis=4)
    denom_second = jnp.sum(jones_product(behind, adjoint(behind)), axis=4)
    from_first = jnp.concatenate([numer_first.reshape(8, chan_count, base_count), denom_first.reshape(8, chan_count, base_count)])
    from_second = jnp.concatenate([numer_second.reshape(8, chan_count, base_count), denom_second.reshape(8, chan_count, base_count)])
    total = jnp.zeros((16, chan_count, stat_count), jnp.float32)
    return total.at[:, :, first].add(from_first).at[:, :, second].add(from_second)


def update(total, old):
    shape = old.shape
    numer = total[:8].reshape(shape)
    denom = total[8:].reshape(shape)
    upper = denom[0, 0, 0] + RIDGE
    lower = denom[0, 1, 1] + RIDGE
    off_real = denom[0, 0, 1]
    off_imag = denom[1, 0, 1]
    determinant = upper * lower - off_real * off_real - off_imag * off_imag
    zero = jnp.zeros_like(upper)
    inverse = jnp.stack([jnp.stack([jnp.stack([lower, -off_real]), jnp.stack([-off_real, upper])]),
                         jnp.stack([jnp.stack([zero, -off_imag]), jnp.stack([off_imag, zero])])]) / determinant
    return 0.5 * (jones_product(numer, inverse) + old)


def smooth(jones):
    shape = jones.shape
    flat = jones.reshape(8, shape[3], shape[4])
    padded = jnp.pad(flat, ((0, 0), (1, 1), (0, 0)))
    total = padded[:, :-2] + 2.0 * padded[:, 1:-1] + padded[:, 2:]
    index = jnp.arange(shape[3])
    weight = 4.0 - (index == 0).astype(jnp.float32) - (index == NC - 1).astype(jnp.float32)
    return (total / weight[None, :, None]).reshape(shape)


def reference(visibility, model_vis, station_pairs, init_gains):
    first = station_pairs[0]
    second = station_pairs[1]
    jones = init_gains.reshape(2, 2, 2, NC, NS)
    vis_lead = jnp.moveaxis(visibility, 1, 0)
    model_lead = jnp.moveaxis(model_vis, 1, 0)
    for step in range(ITERS):
        jones_lead = jnp.moveaxis(jones, 3, 0)

        def per_channel(items):
            vis_one, model_one, jones_one = items
            return station_terms(vis_one.reshape(2, 2, 2, 1, NT, NB), model_one.reshape(2, 2, 2, 1, NT, NB),
                                 jones_one.reshape(2, 2, 2, 1, NS), first, second, NS)[:, 0, :]

        sums = lax.map(per_channel, (vis_lead, model_lead, jones_lead))
        total = jnp.moveaxis(sums, 0, 1)
        jones = smooth(update(total, jones))
    return jones.reshape(8, NC, NS)
```

```python
import jax
import jax.numpy as jnp
from jax import lax
from jax.experimental import pallas as pl
from jax.experimental.pallas import tpu as pltpu
from jax.sharding import PartitionSpec as P

ITERS = 3
RIDGE = 1.0
NX, NZ, NCH = 4, 8, 8
NS, NB = 512, 4096
LANES = 128
MESH = pl.DeviceIdType.MESH
F32, BF16 = jnp.float32, jnp.bfloat16


def hops(off):
    return min(off[0], NX - off[0]) + min(off[1], NZ - off[1])


OFFSETS = sorted([(i, j) for i in range(NX) for j in range(NZ)], key=lambda o: -hops(o))
PEERS = [o for o in OFFSETS if o != (0, 0)]


def cmul(a, b, ca=False, cb=False):
    (ar, ai), (br, bi) = a, b
    re = ar * br + ai * bi if ca != cb else ar * br - ai * bi
    if ca:
        im = ar * bi - ai * br if not cb else -(ar * bi + ai * br)
    else:
        im = ai * br - ar * bi if cb else ar * bi + ai * br
    return re, im


def cadd(a, b):
    return a[0] + b[0], a[1] + b[1]


def mm(a, b, ah=False, bh=False):
    def one(i, j):
        parts = []
        for k in range(2):
            left = a[k][i] if ah else a[i][k]
            right = b[j][k] if bh else b[k][j]
            parts.append(cmul(left, right, ah, bh))
        return cadd(*parts)

    return [[one(i, j) for j in range(2)] for i in range(2)]


def herm(a):
    def square(z):
        return z[0] * z[0] + z[1] * z[1]

    off = cadd(cmul(a[0][0], a[1][0], cb=True), cmul(a[0][1], a[1][1], cb=True))
    return [square(a[0][0]) + square(a[0][1]), square(a[1][0]) + square(a[1][1]), off[0], off[1]]


def mat(v):
    return [[(v[2 * i + j], v[4 + 2 * i + j]) for j in range(2)] for i in range(2)]


def flat(m):
    return [m[i][j][p] for p in range(2) for i in range(2) for j in range(2)]


def station_terms(vis, model, gain_first, gain_second):
    total = None
    for t in range(2):
        v, m = mat(vis[t]), mat(model[t])
        ahead = mm(m, gain_second, bh=True)
        behind = mm(m, gain_first, ah=True, bh=True)
        new = [
            flat(mm(v, ahead, bh=True)) + herm(ahead),
            flat(mm(v, behind, ah=True, bh=True)) + herm(behind),
        ]
        total = new if total is None else [[x + y for x, y in zip(s, n)] for s, n in zip(total, new)]
    return total


def kernel(vis_hbm, model_hbm, pairs, init, out, vis, model, table_g, table_s, gains_lhs, gains, terms, acc, gs, sb, rb, gb, mine, in_sem, rs_send, rs_recv, ag_send, ag_recv):
    c, b = lax.axis_index("chan"), lax.axis_index("bl")
    x, z = b // NZ, b % NZ
    my_ch = lax.rem(z + 2 * x, NCH)

    def peer(off, dc=0):
        dx, dz = off
        return (lax.rem(c + dc + 8, 8), lax.rem(x + dx, NX) * NZ + lax.rem(z + dz, NZ))

    barrier = pltpu.get_barrier_semaphore()

    def greet(device):
        pl.semaphore_signal(barrier, inc=1, device_id=device, device_id_type=MESH)

    for i in range(NX):
        greet((lax.rem(c + 1, 8), i * NZ + lax.rem(16 - 2 * i, NZ)))
        greet((lax.rem(c + 7, 8), i * NZ + lax.rem(23 - 2 * i, NZ)))
    for off in PEERS:
        greet(peer(off))

    copies = []
    for t in range(2):
        for k in range(NCH):
            copies.append(pltpu.make_async_copy(vis_hbm.at[:, k, t, :], vis.at[t, :, k, :], in_sem.at[2 * NCH * t + k]))
            copies.append(pltpu.make_async_copy(model_hbm.at[:, k, t, :], model.at[t, :, k, :], in_sem.at[2 * NCH * t + NCH + k]))
    for copy in copies:
        copy.start()

    low = lax.broadcasted_iota(jnp.int32, (256, LANES), 0)
    wide = lax.broadcasted_iota(jnp.int32, (LANES, NS), 1).astype(F32)
    for side in range(2):

        def tables(g, _):
            lanes = pl.ds(pl.multiple_of(g * LANES, LANES), LANES)
            dst = pl.ds(pl.multiple_of(side * NB + g * LANES, LANES), LANES)
            row = pairs[side : side + 1, lanes]
            table_g[:, dst] = jnp.where(jnp.broadcast_to(row & 255, (256, LANES)) == low, 1.0, 0.0).astype(BF16)
            column = jnp.broadcast_to(row.astype(F32), (LANES, LANES)).T
            column = jnp.concatenate([column] * 4, axis=1)
            table_s[dst, :] = jnp.where(column == wide, 1.0, 0.0).astype(BF16)
            return 0

        lax.fori_loop(0, NB // LANES, tables, 0)

    for s in range(4):
        for k in range(8):
            gs[pl.ds(s * 64 + k, 8, stride=8), :] = init[k, :, s * LANES : (s + 1) * LANES]

    for copy in copies:
        copy.wait()

    def iteration(step, _):
        for s in range(4):
            rows, lanes = (s // 2) * 128, slice((s % 2) * LANES, (s % 2 + 1) * LANES)
            for k in range(0, 8, 2):
                two = jnp.concatenate([gs[pl.ds(s * 64 + k + i, 8, stride=8), :] for i in range(2)], axis=0)
                high = two.astype(BF16)
                gains_lhs[rows + 8 * k : rows + 8 * k + 16, lanes] = high
                gains_lhs[rows + 64 + 8 * k : rows + 64 + 8 * k + 16, lanes] = (two - high.astype(F32)).astype(BF16)

        width = 1024
        for side in range(2):

            def lookup(g, _):
                src = pl.ds(pl.multiple_of(g * width, width), width)
                dst = pl.ds(pl.multiple_of(side * NB + g * width, width), width)
                picked = jnp.dot(gains_lhs[...], table_g[:, dst], preferred_element_type=F32)
                upper = jnp.broadcast_to(pairs[side : side + 1, src], (128, width)) >= 256
                picked = jnp.where(upper, picked[128:], picked[:128])
                gains[:, dst] = picked[:64] + picked[64:]
                return 0

            lax.fori_loop(0, NB // width, lookup, 0)

        def compute(g, _):
            lanes = pl.ds(pl.multiple_of(g * LANES, LANES), LANES)
            later = pl.ds(pl.multiple_of(NB + g * LANES, LANES), LANES)
            v = [[vis[t, k, :, lanes] for k in range(8)] for t in range(2)]
            m = [[model[t, k, :, lanes] for k in range(8)] for t in range(2)]
            first = mat([gains[8 * k : 8 * k + 8, lanes] for k in range(8)])
            second = mat([gains[8 * k : 8 * k + 8, later] for k in range(8)])
            for dst, term in zip((lanes, later), station_terms(v, m, first, second)):
                for k in range(0, 12, 2):
                    two = jnp.concatenate([term[k], term[k + 1]], axis=0)
                    high = two.astype(BF16)
                    terms[8 * k : 8 * k + 16, dst] = high
                    terms[96 + 8 * k : 96 + 8 * k + 16, dst] = (two - high.astype(F32)).astype(BF16)
            return 0

        lax.fori_loop(0, NB // LANES, compute, 0)

        for n in range(2):
            half = slice(n * 256, n * 256 + 256)
            both = jnp.dot(terms[...], table_s[:, half], preferred_element_type=F32)
            both = both[:96] + both[96:]
            for s in range(2):
                acc[2 * n + s] = both[:, s * LANES : (s + 1) * LANES]
        for s in range(4):
            for k in range(NCH):
                sb[step, s, k] = acc[s, pl.ds(k, 12, stride=8), :]

        @pl.when(step == 0)
        def _():
            edge = jnp.where((my_ch == 0) | (my_ch == NCH - 1), 32, 0)
            pl.semaphore_wait(barrier, 31 + edge)

        for off in PEERS:
            there = peer(off)[1]
            tx, tz = there // NZ, there % NZ
            pltpu.make_async_remote_copy(
                src_ref=sb.at[step, tx, lax.rem(tz + 2 * tx, NCH)],
                dst_ref=rb.at[step, b],
                send_sem=rs_send.at[step],
                recv_sem=rs_recv.at[step],
                device_id=peer(off),
                device_id_type=MESH,
            ).start()
        rb[step, b] = sb[step, x, my_ch]
        landed = rb.at[step, pl.ds(0, 31)]
        pltpu.make_async_copy(landed, landed, rs_recv.at[step]).wait()

        total = rb[step, 0]
        for i in range(1, 32):
            total = total + rb[step, i]
        row = [total[k : k + 1, :] for k in range(12)]
        numer = mat(row[:8])
        upper, lower = row[8] + RIDGE, row[9] + RIDGE
        off_real, off_imag = row[10], row[11]
        inv = 1.0 / (upper * lower - off_real * off_real - off_imag * off_imag)
        zero = jnp.zeros_like(upper)
        inverse = [
            [(lower * inv, zero), (-off_real * inv, -off_imag * inv)],
            [(-off_real * inv, off_imag * inv), (upper * inv, zero)],
        ]
        old = gs[pl.ds(pl.multiple_of(x * 64 + my_ch * 8, 8), 8), :]
        solved = jnp.concatenate(flat(mm(numer, inverse)), axis=0)
        mine[step] = 0.5 * (solved + old)
        slot = x * 10 + my_ch + 1
        gb[step, slot] = mine[step]

        def give(device, there):
            pltpu.make_async_remote_copy(
                src_ref=mine.at[step],
                dst_ref=gb.at[step, there],
                send_sem=ag_send.at[step],
                recv_sem=ag_recv.at[step],
                device_id=device,
                device_id_type=MESH,
            ).start()

        @pl.when(my_ch == 0)
        def _():
            for off in OFFSETS:
                give(peer(off, -1), x * 10 + 9)

        @pl.when(my_ch == NCH - 1)
        def _():
            for off in OFFSETS:
                give(peer(off, 1), x * 10)

        for off in PEERS:
            give(peer(off), slot)
        landed = gb.at[step, pl.ds(0, 39)]
        pltpu.make_async_copy(landed, landed, ag_recv.at[step]).wait()

        for s in range(4):
            edge_before = jnp.where(c == 0, 0.0, gb[step, s * 10])
            edge_after = jnp.where(c == 7, 0.0, gb[step, s * 10 + 9])
            near = [edge_before] + [gb[step, s * 10 + k] for k in range(1, 9)] + [edge_after]
            for k in range(NCH):
                total = near[k] + 2.0 * near[k + 1] + near[k + 2]
                weight = 0.25
                if k == 0:
                    weight = jnp.where(c == 0, 1.0 / 3.0, 0.25)
                if k == NCH - 1:
                    weight = jnp.where(c == 7, 1.0 / 3.0, 0.25)
                gs[s * 64 + 8 * k : s * 64 + 8 * k + 8, :] = total * weight

        gone = rb.at[step, pl.ds(0, 31)]
        pltpu.make_async_copy(gone, gone, rs_send.at[step]).wait()
        gone = gb.at[step, pl.ds(0, 31)]
        pltpu.make_async_copy(gone, gone, ag_send.at[step]).wait()

        @pl.when((my_ch == 0) | (my_ch == NCH - 1))
        def _():
            gone = gb.at[step, pl.ds(0, 32)]
            pltpu.make_async_copy(gone, gone, ag_send.at[step]).wait()

        return 0

    lax.fori_loop(0, ITERS, iteration, 0)
    for s in range(4):
        for k in range(8):
            out[k, :, s * LANES : (s + 1) * LANES] = gs[pl.ds(s * 64 + k, 8, stride=8), :]


def body(visibility, model_vis, station_pairs, init_gains):
    vmem = pl.BlockSpec(memory_space=pltpu.VMEM)
    hbm = pl.BlockSpec(memory_space=pl.ANY)
    return pl.pallas_call(
        kernel,
        out_shape=jax.ShapeDtypeStruct((8, NCH, NS), F32),
        in_specs=[hbm, hbm, vmem, vmem],
        out_specs=vmem,
        scratch_shapes=[
            pltpu.VMEM((2, 8, NCH, NB), F32),
            pltpu.VMEM((2, 8, NCH, NB), F32),
            pltpu.VMEM((256, 2 * NB), BF16),
            pltpu.VMEM((2 * NB, NS), BF16),
            pltpu.VMEM((256, 256), BF16),
            pltpu.VMEM((64, 2 * NB), F32),
            pltpu.VMEM((192, 2 * NB), BF16),
            pltpu.VMEM((4, 96, LANES), F32),
            pltpu.VMEM((256, LANES), F32),
            pltpu.VMEM((ITERS, 4, NCH, 12, LANES), F32),
            pltpu.VMEM((ITERS, 32, 12, LANES), F32),
            pltpu.VMEM((ITERS, 40, 8, LANES), F32),
            pltpu.VMEM((ITERS, 8, LANES), F32),
            pltpu.SemaphoreType.DMA((32,)),
            pltpu.SemaphoreType.DMA((ITERS,)),
            pltpu.SemaphoreType.DMA((ITERS,)),
            pltpu.SemaphoreType.DMA((ITERS,)),
            pltpu.SemaphoreType.DMA((ITERS,)),
        ],
        compiler_params=pltpu.CompilerParams(collective_id=0, has_side_effects=True, vmem_limit_bytes=56 << 20),
    )(visibility, model_vis, station_pairs, init_gains)


def solution(mesh):
    in_specs = (
        P(None, "chan", None, "bl"),
        P(None, "chan", None, "bl"),
        P(None, "bl"),
        P(None, "chan", None),
    )
    return jax.shard_map(body, mesh=mesh, in_specs=in_specs, out_specs=P(None, "chan", None), check_vma=False)
```

```python
import functools

import jax
import jax.numpy as jnp
from jax import lax
from jax.experimental import pallas as pl
from jax.experimental.pallas import tpu as pltpu
from jax.sharding import PartitionSpec as P

ITERS = 3
RIDGE = 1.0
NX, NZ, NCH = 4, 8, 8
NS, NB = 512, 4096
LANES = 128
W = 1024
CHUNKS = NB // W
MESH = pl.DeviceIdType.MESH
F32, BF16 = jnp.float32, jnp.bfloat16


def hops(off):
    return min(off[0], NX - off[0]) + min(off[1], NZ - off[1])


OFFSETS = sorted([(i, j) for i in range(NX) for j in range(NZ)], key=lambda o: -hops(o))
PEERS = [o for o in OFFSETS if o != (0, 0)]


def cmul(a, b, ca=False, cb=False):
    (ar, ai), (br, bi) = a, b
    re = ar * br + ai * bi if ca != cb else ar * br - ai * bi
    if ca:
        im = ar * bi - ai * br if not cb else -(ar * bi + ai * br)
    else:
        im = ai * br - ar * bi if cb else ar * bi + ai * br
    return re, im


def cadd(a, b):
    return a[0] + b[0], a[1] + b[1]


def mm(a, b, ah=False, bh=False):
    def one(i, j):
        parts = []
        for k in range(2):
            left = a[k][i] if ah else a[i][k]
            right = b[j][k] if bh else b[k][j]
            parts.append(cmul(left, right, ah, bh))
        return cadd(*parts)

    return [[one(i, j) for j in range(2)] for i in range(2)]


def square(z):
    return z[0] * z[0] + z[1] * z[1]


def tree(terms):
    while len(terms) > 1:
        terms = [terms[i] + terms[i + 1] for i in range(0, len(terms), 2)]
    return terms[0]


def mat(v):
    return [[(v[2 * i + j], v[4 + 2 * i + j]) for j in range(2)] for i in range(2)]


def flat(m):
    return [m[i][j][p] for p in range(2) for i in range(2) for j in range(2)]


def over_time(one):
    return cadd(one(0), one(1))


def products(vis, model):
    v, m = [mat(a) for a in vis], [mat(a) for a in model]
    numer = [
        over_time(lambda t: cmul(v[t][i][j], m[t][l][k], cb=True))
        for i in range(2) for j in range(2) for l in range(2) for k in range(2)
    ]

    def cross(a, b):
        return over_time(lambda t: cmul(m[t][a[0]][a[1]], m[t][b[0]][b[1]], cb=True))

    power = [square(m[0][i][j]) + square(m[1][i][j]) for i in range(2) for j in range(2)]
    u, w = cross((0, 0), (1, 1)), cross((0, 1), (1, 0))
    pairs = [cross((0, 0), (0, 1)), cross((1, 0), (1, 1)), cross((0, 0), (1, 0)), cross((0, 1), (1, 1))]
    mixed = [u[0] + w[0], w[1] - u[1], u[1] + w[1], u[0] - w[0]]
    return numer, power + [part for pair in pairs for part in pair] + mixed


def side_terms(side, numer, denom, gain):
    rows = []
    for i in range(2):
        for l in range(2):
            re, im = [], []
            for j in range(2):
                for k in range(2):
                    cr, ci = numer(i, j, l, k) if side == 0 else numer(j, i, k, l)
                    gr, gi = gain[j][k]
                    if side == 0:
                        re.append(cr * gr - ci * gi)
                        im.append(cr * gi + ci * gr)
                    else:
                        re.append(cr * gr + ci * gi)
                        im.append(cr * gi - ci * gr)
            rows.append((tree(re), tree(im)))
    out = [r[0] for r in rows] + [r[1] for r in rows]
    h00, h11 = square(gain[0][0]) + square(gain[1][0]), square(gain[0][1]) + square(gain[1][1])
    hr, hi = cadd(cmul(gain[0][0], gain[0][1], ca=True), cmul(gain[1][0], gain[1][1], ca=True))
    h2r, h2i = hr + hr, hi + hi
    d = [denom(n) for n in range(16)]
    if side == 0:
        out.append((d[0] * h00 + d[1] * h11) + (d[4] * h2r - d[5] * h2i))
        out.append((d[2] * h00 + d[3] * h11) + (d[6] * h2r - d[7] * h2i))
        out.append((d[8] * h00 + d[10] * h11) + (d[12] * hr + d[13] * hi))
        out.append((d[9] * h00 + d[11] * h11) + (d[14] * hr + d[15] * hi))
    else:
        out.append((d[0] * h00 + d[2] * h11) + (d[8] * h2r + d[9] * h2i))
        out.append((d[1] * h00 + d[3] * h11) + (d[10] * h2r + d[11] * h2i))
        out.append((d[4] * h00 + d[6] * h11) + (d[12] * hr + d[14] * hi))
        out.append((d[13] * hr + d[15] * hi) - (d[5] * h00 + d[7] * h11))
    return out


def kernel(vis_hbm, model_hbm, pairs, init, out, vis, model, numer, denom, table, table_t, gains_lhs, gains0, gains1, terms0, terms1, acc, acc4, gs, sb, rb, gb, mine, in_sem, rs_send, rs_recv, ag_send, ag_recv):
    c, b = lax.axis_index("chan"), lax.axis_index("bl")
    x, z = b // NZ, b % NZ
    def owned(x, z, c):
        place = lax.rem(z + x + 2 * (c % 2), NCH)
        return jnp.where(place < 4, place, jnp.where(place == 4, NCH - 1, place - 1))

    def edge_owner(x, c, last):
        return lax.rem(16 + 4 * last - x - 2 * (c % 2), NZ)

    my_ch = owned(x, z, c)

    def peer(off, dc=0):
        dx, dz = off
        return (lax.rem(c + dc + 8, 8), lax.rem(x + dx, NX) * NZ + lax.rem(z + dz, NZ))

    barrier = pltpu.get_barrier_semaphore()

    def greet(device):
        pl.semaphore_signal(barrier, inc=1, device_id=device, device_id_type=MESH)

    for i in range(NX):
        greet((lax.rem(c + 1, 8), i * NZ + edge_owner(i, c + 1, 0)))
        greet((lax.rem(c + 7, 8), i * NZ + edge_owner(i, c + 1, 1)))
    for off in PEERS:
        greet(peer(off))

    copies = []
    for t in range(2):
        for k in range(NCH):
            copies.append(pltpu.make_async_copy(vis_hbm.at[:, k, t, :], vis.at[t, :, k, :], in_sem.at[2 * NCH * t + k]))
            copies.append(pltpu.make_async_copy(model_hbm.at[:, k, t, :], model.at[t, :, k, :], in_sem.at[2 * NCH * t + NCH + k]))
    for copy in copies:
        copy.start()

    low = lax.broadcasted_iota(jnp.int32, (256, LANES), 0).astype(F32).astype(BF16)
    one, nil = jnp.ones((256, LANES), BF16), jnp.zeros((256, LANES), BF16)
    across = lax.broadcasted_iota(jnp.int32, (LANES, 256), 1).astype(F32).astype(BF16)
    one_t, nil_t = jnp.ones((LANES, 256), BF16), jnp.zeros((LANES, 256), BF16)

    def tables(g, _):
        src = pl.ds(pl.multiple_of(g * LANES, LANES), LANES)
        for side in range(2):
            per = W // LANES
            dst = pl.ds(pl.multiple_of((2 * (g // per) + side) * W + g % per * LANES, LANES), LANES)
            station = pairs[side : side + 1, src]
            row = (station & 255).astype(F32)
            rows = jnp.concatenate([jnp.broadcast_to(row, (16, LANES)).astype(BF16)] * 16, axis=0)
            table[:, dst] = jnp.where(rows == low, one, nil)
            for half in range(2):
                inside = station >= 256 if half else station < 256
                column = jnp.broadcast_to(jnp.where(inside, row, -1.0), (LANES, LANES)).T.astype(BF16)
                column = jnp.concatenate([column] * 2, axis=1)
                table_t[dst, half * 256 : half * 256 + 256] = jnp.where(column == across, one_t, nil_t)
        return 0

    lax.fori_loop(0, NB // LANES, tables, 0)

    for s in range(4):
        for k in range(8):
            gs[pl.ds(s * 64 + k, 8, stride=8), :] = init[k, :, s * LANES : (s + 1) * LANES]

    for copy in copies:
        copy.wait()

    def prepare(g, _):
        lanes = pl.ds(pl.multiple_of(g * LANES, LANES), LANES)
        v = [[vis[t, k, :, lanes] for k in range(8)] for t in range(2)]
        m = [[model[t, k, :, lanes] for k in range(8)] for t in range(2)]
        for_numer, for_denom = products(v, m)
        for n in range(16):
            numer[0, n, :, lanes] = for_numer[n][0]
            numer[1, n, :, lanes] = for_numer[n][1]
            denom[n, :, lanes] = for_denom[n]
        return 0

    lax.fori_loop(0, NB // LANES, prepare, 0)

    def iteration(step, _):
        for s in range(4):
            rows, lanes = (s // 2) * 128, slice((s % 2) * LANES, (s % 2 + 1) * LANES)
            for k in range(0, 8, 2):
                two = jnp.concatenate([gs[pl.ds(s * 64 + k + i, 8, stride=8), :] for i in range(2)], axis=0)
                high = two.astype(BF16)
                gains_lhs[rows + 8 * k : rows + 8 * k + 16, lanes] = high
                gains_lhs[rows + 64 + 8 * k : rows + 64 + 8 * k + 16, lanes] = (two - high.astype(F32)).astype(BF16)

        def lookup(i, side, gains):
            picked = jnp.dot(gains_lhs[...], table[:, (2 * i + side) * W : (2 * i + side + 1) * W], preferred_element_type=F32)
            for g in range(W // LANES):
                lanes = slice(i * W + g * LANES, i * W + (g + 1) * LANES)
                at = slice(g * LANES, (g + 1) * LANES)
                upper = jnp.broadcast_to(pairs[side : side + 1, lanes], (128, LANES)) >= 256
                chosen = jnp.where(upper, picked[128:, at], picked[:128, at])
                gains[:, side * W + g * LANES : side * W + (g + 1) * LANES] = chosen[:64] + chosen[64:]

        def compute(i, side, g, gains, terms):
            lanes = slice(i * W + g * LANES, i * W + (g + 1) * LANES)
            here = slice(side * W + g * LANES, side * W + (g + 1) * LANES)
            other = slice((1 - side) * W + g * LANES, (1 - side) * W + (g + 1) * LANES)
            gain = mat([gains[8 * k : 8 * k + 8, other] for k in range(8)])

            def pick(i, j, l, k):
                n = 8 * i + 4 * j + 2 * l + k
                return numer[0, n, :, lanes], numer[1, n, :, lanes]

            term = side_terms(side, pick, lambda n: denom[n, :, lanes], gain)
            for k in range(0, 12, 2):
                two = jnp.concatenate([term[k], term[k + 1]], axis=0)
                high = two.astype(BF16)
                terms[8 * k : 8 * k + 16, here] = high
                terms[96 + 8 * k : 112 + 8 * k, here] = (two - high.astype(F32)).astype(BF16)

        def collect(i, half, terms):
            columns = slice(half * 256, half * 256 + 256)
            found = jnp.dot(terms[...], table_t[2 * i * W : 2 * (i + 1) * W, columns], preferred_element_type=F32)
            if i == 0:
                acc[:, columns] = found
            else:
                acc[:, columns] += found

        gains, terms = (gains0, gains1), (terms0, terms1)
        for side in range(2):
            lookup(0, side, gains0)
        for i in range(CHUNKS):
            matrix = []
            if i + 1 < CHUNKS:
                matrix += [functools.partial(lookup, i + 1, side, gains[(i + 1) % 2]) for side in range(2)]
            if i > 0:
                matrix += [functools.partial(collect, i - 1, half, terms[(i + 1) % 2]) for half in range(2)]
            vector = [(side, g) for g in range(W // LANES) for side in range(2)]
            share = len(vector) // len(matrix)
            for n, part in enumerate(matrix):
                part()
                for side, g in vector[n * share : (n + 1) * share]:
                    compute(i, side, g, gains[i % 2], terms[i % 2])
        for half in range(2):
            collect(CHUNKS - 1, half, terms[(CHUNKS - 1) % 2])
        for s in range(4):
            lanes = slice(s * LANES, (s + 1) * LANES)
            acc4[s] = acc[:96, lanes] + acc[96:, lanes]
        for s in range(4):
            for k in range(NCH):
                sb[step, s, k] = acc4[s, pl.ds(k, 12, stride=8), :]

        @pl.when(step == 0)
        def _():
            edge = jnp.where((my_ch == 0) | (my_ch == NCH - 1), 32, 0)
            pl.semaphore_wait(barrier, 31 + edge)

        for off in PEERS:
            there = peer(off)[1]
            tx, tz = there // NZ, there % NZ
            pltpu.make_async_remote_copy(
                src_ref=sb.at[step, tx, owned(tx, tz, c)],
                dst_ref=rb.at[step, b],
                send_sem=rs_send.at[step],
                recv_sem=rs_recv.at[step],
                device_id=peer(off),
                device_id_type=MESH,
            ).start()
        rb[step, b] = sb[step, x, my_ch]
        landed = rb.at[step, pl.ds(0, 31)]
        pltpu.make_async_copy(landed, landed, rs_recv.at[step]).wait()

        total = rb[step, 0]
        for i in range(1, 32):
            total = total + rb[step, i]
        row = [total[k : k + 1, :] for k in range(12)]
        num = mat(row[:8])
        upper, lower = row[8] + RIDGE, row[9] + RIDGE
        off_real, off_imag = row[10], row[11]
        inv = 1.0 / (upper * lower - off_real * off_real - off_imag * off_imag)
        zero = jnp.zeros_like(upper)
        inverse = [
            [(lower * inv, zero), (-off_real * inv, -off_imag * inv)],
            [(-off_real * inv, off_imag * inv), (upper * inv, zero)],
        ]
        old = gs[pl.ds(pl.multiple_of(x * 64 + my_ch * 8, 8), 8), :]
        solved = jnp.concatenate(flat(mm(num, inverse)), axis=0)
        mine[step] = 0.5 * (solved + old)
        slot = x * 10 + my_ch + 1
        gb[step, slot] = mine[step]

        def give(device, there):
            pltpu.make_async_remote_copy(
                src_ref=mine.at[step],
                dst_ref=gb.at[step, there],
                send_sem=ag_send.at[step],
                recv_sem=ag_recv.at[step],
                device_id=device,
                device_id_type=MESH,
            ).start()

        for ch, dc, there in ((0, -1, x * 10 + 9), (NCH - 1, 1, x * 10)):

            @pl.when(my_ch == ch)
            def _():
                for far in range(7, -1, -1):
                    for off in OFFSETS:
                        if hops(off) + 1 == far:
                            give(peer(off, dc), there)
                        if hops(off) == far and far > 0:
                            give(peer(off), slot)

        @pl.when((my_ch > 0) & (my_ch < NCH - 1))
        def _():
            for off in PEERS:
                give(peer(off), slot)

        landed = gb.at[step, pl.ds(0, 39)]
        pltpu.make_async_copy(landed, landed, ag_recv.at[step]).wait()

        for s in range(4):
            edge_before = jnp.where(c == 0, 0.0, gb[step, s * 10])
            edge_after = jnp.where(c == 7, 0.0, gb[step, s * 10 + 9])
            near = [edge_before] + [gb[step, s * 10 + k] for k in range(1, 9)] + [edge_after]
            for k in range(NCH):
                total = near[k] + 2.0 * near[k + 1] + near[k + 2]
                weight = 0.25
                if k == 0:
                    weight = jnp.where(c == 0, 1.0 / 3.0, 0.25)
                if k == NCH - 1:
                    weight = jnp.where(c == 7, 1.0 / 3.0, 0.25)
                gs[s * 64 + 8 * k : s * 64 + 8 * k + 8, :] = total * weight

        gone = rb.at[step, pl.ds(0, 31)]
        pltpu.make_async_copy(gone, gone, rs_send.at[step]).wait()
        gone = gb.at[step, pl.ds(0, 31)]
        pltpu.make_async_copy(gone, gone, ag_send.at[step]).wait()

        @pl.when((my_ch == 0) | (my_ch == NCH - 1))
        def _():
            gone = gb.at[step, pl.ds(0, 32)]
            pltpu.make_async_copy(gone, gone, ag_send.at[step]).wait()

        return 0

    lax.fori_loop(0, ITERS, iteration, 0)
    for s in range(4):
        for k in range(8):
            out[k, :, s * LANES : (s + 1) * LANES] = gs[pl.ds(s * 64 + k, 8, stride=8), :]


def body(visibility, model_vis, station_pairs, init_gains):
    vmem = pl.BlockSpec(memory_space=pltpu.VMEM)
    hbm = pl.BlockSpec(memory_space=pl.ANY)
    return pl.pallas_call(
        kernel,
        out_shape=jax.ShapeDtypeStruct((8, NCH, NS), F32),
        in_specs=[hbm, hbm, vmem, vmem],
        out_specs=vmem,
        scratch_shapes=[
            pltpu.VMEM((2, 8, NCH, NB), F32),
            pltpu.VMEM((2, 8, NCH, NB), F32),
            pltpu.VMEM((2, 16, NCH, NB), F32),
            pltpu.VMEM((16, NCH, NB), F32),
            pltpu.VMEM((256, 2 * NB), BF16),
            pltpu.VMEM((2 * NB, NS), BF16),
            pltpu.VMEM((256, 256), BF16),
            pltpu.VMEM((64, 2 * W), F32),
            pltpu.VMEM((64, 2 * W), F32),
            pltpu.VMEM((192, 2 * W), BF16),
            pltpu.VMEM((192, 2 * W), BF16),
            pltpu.VMEM((192, NS), F32),
            pltpu.VMEM((4, 96, LANES), F32),
            pltpu.VMEM((256, LANES), F32),
            pltpu.VMEM((ITERS, 4, NCH, 12, LANES), F32),
            pltpu.VMEM((ITERS, 32, 12, LANES), F32),
            pltpu.VMEM((ITERS, 40, 8, LANES), F32),
            pltpu.VMEM((ITERS, 8, LANES), F32),
            pltpu.SemaphoreType.DMA((32,)),
            pltpu.SemaphoreType.DMA((ITERS,)),
            pltpu.SemaphoreType.DMA((ITERS,)),
            pltpu.SemaphoreType.DMA((ITERS,)),
            pltpu.SemaphoreType.DMA((ITERS,)),
        ],
        compiler_params=pltpu.CompilerParams(collective_id=0, has_side_effects=True, vmem_limit_bytes=56 << 20),
    )(visibility, model_vis, station_pairs, init_gains)


def solution(mesh):
    in_specs = (
        P(None, "chan", None, "bl"),
        P(None, "chan", None, "bl"),
        P(None, "bl"),
        P(None, "chan", None),
    )
    return jax.shard_map(body, mesh=mesh, in_specs=in_specs, out_specs=P(None, "chan", None), check_vma=False)
```

```python
import functools

import jax
import jax.numpy as jnp
from jax import lax
from jax.experimental import pallas as pl
from jax.experimental.pallas import tpu as pltpu
from jax.sharding import PartitionSpec as P

ITERS = 3
RIDGE = 1.0
NX, NZ, NCH = 4, 8, 8
NS, NB = 512, 4096
LANES = 128
W = 1024
CHUNKS = NB // W
MESH = pl.DeviceIdType.MESH
F32, BF16 = jnp.float32, jnp.bfloat16


def hops(off):
    return min(off[0], NX - off[0]) + min(off[1], NZ - off[1])


OFFSETS = sorted([(i, j) for i in range(NX) for j in range(NZ)], key=lambda o: -hops(o))
PEERS = [o for o in OFFSETS if o != (0, 0)]


def cmul(a, b, ca=False, cb=False):
    (ar, ai), (br, bi) = a, b
    re = ar * br + ai * bi if ca != cb else ar * br - ai * bi
    if ca:
        im = ar * bi - ai * br if not cb else -(ar * bi + ai * br)
    else:
        im = ai * br - ar * bi if cb else ar * bi + ai * br
    return re, im


def cadd(a, b):
    return a[0] + b[0], a[1] + b[1]


def mm(a, b, ah=False, bh=False):
    def one(i, j):
        parts = []
        for k in range(2):
            left = a[k][i] if ah else a[i][k]
            right = b[j][k] if bh else b[k][j]
            parts.append(cmul(left, right, ah, bh))
        return cadd(*parts)

    return [[one(i, j) for j in range(2)] for i in range(2)]


def square(z):
    return z[0] * z[0] + z[1] * z[1]


def tree(terms):
    while len(terms) > 1:
        terms = [terms[i] + terms[i + 1] for i in range(0, len(terms), 2)]
    return terms[0]


def mat(v):
    return [[(v[2 * i + j], v[4 + 2 * i + j]) for j in range(2)] for i in range(2)]


def flat(m):
    return [m[i][j][p] for p in range(2) for i in range(2) for j in range(2)]


def over_time(one):
    return cadd(one(0), one(1))


def products(vis, model):
    v, m = [mat(a) for a in vis], [mat(a) for a in model]
    numer = [
        over_time(lambda t: cmul(v[t][i][j], m[t][l][k], cb=True))
        for i in range(2) for j in range(2) for l in range(2) for k in range(2)
    ]

    def cross(a, b):
        return over_time(lambda t: cmul(m[t][a[0]][a[1]], m[t][b[0]][b[1]], cb=True))

    power = [square(m[0][i][j]) + square(m[1][i][j]) for i in range(2) for j in range(2)]
    u, w = cross((0, 0), (1, 1)), cross((0, 1), (1, 0))
    pairs = [cross((0, 0), (0, 1)), cross((1, 0), (1, 1)), cross((0, 0), (1, 0)), cross((0, 1), (1, 1))]
    mixed = [u[0] + w[0], w[1] - u[1], u[1] + w[1], u[0] - w[0]]
    return numer, power + [part for pair in pairs for part in pair] + mixed


def side_terms(side, numer, denom, gain):
    rows = []
    for i in range(2):
        for l in range(2):
            re, im = [], []
            for j in range(2):
                for k in range(2):
                    cr, ci = numer(i, j, l, k) if side == 0 else numer(j, i, k, l)
                    gr, gi = gain[j][k]
                    if side == 0:
                        re.append(cr * gr - ci * gi)
                        im.append(cr * gi + ci * gr)
                    else:
                        re.append(cr * gr + ci * gi)
                        im.append(cr * gi - ci * gr)
            rows.append((tree(re), tree(im)))
    out = [r[0] for r in rows] + [r[1] for r in rows]
    h00, h11 = square(gain[0][0]) + square(gain[1][0]), square(gain[0][1]) + square(gain[1][1])
    hr, hi = cadd(cmul(gain[0][0], gain[0][1], ca=True), cmul(gain[1][0], gain[1][1], ca=True))
    h2r, h2i = hr + hr, hi + hi
    d = [denom(n) for n in range(16)]
    if side == 0:
        out.append((d[0] * h00 + d[1] * h11) + (d[4] * h2r - d[5] * h2i))
        out.append((d[2] * h00 + d[3] * h11) + (d[6] * h2r - d[7] * h2i))
        out.append((d[8] * h00 + d[10] * h11) + (d[12] * hr + d[13] * hi))
        out.append((d[9] * h00 + d[11] * h11) + (d[14] * hr + d[15] * hi))
    else:
        out.append((d[0] * h00 + d[2] * h11) + (d[8] * h2r + d[9] * h2i))
        out.append((d[1] * h00 + d[3] * h11) + (d[10] * h2r + d[11] * h2i))
        out.append((d[4] * h00 + d[6] * h11) + (d[12] * hr + d[14] * hi))
        out.append((d[13] * hr + d[15] * hi) - (d[5] * h00 + d[7] * h11))
    return out


def kernel(vis_hbm, model_hbm, pairs, init, out, vis, model, numer, denom, table, table_t, gains_lhs, gains0, gains1, terms0, terms1, terms2, terms3, acc, acc4, gs, sb, rb, gb, mine, in_sem, rs_send, rs_recv, ag_send, ag_recv):
    c, b = lax.axis_index("chan"), lax.axis_index("bl")
    x, z = b // NZ, b % NZ
    def owned(x, z, c):
        place = lax.rem(z + x + 2 * (c % 2), NCH)
        return jnp.where(place < 4, place, jnp.where(place == 4, NCH - 1, place - 1))

    def edge_owner(x, c, last):
        return lax.rem(16 + 4 * last - x - 2 * (c % 2), NZ)

    my_ch = owned(x, z, c)

    def peer(off, dc=0):
        dx, dz = off
        return (lax.rem(c + dc + 8, 8), lax.rem(x + dx, NX) * NZ + lax.rem(z + dz, NZ))

    barrier = pltpu.get_barrier_semaphore()

    def greet(device):
        pl.semaphore_signal(barrier, inc=1, device_id=device, device_id_type=MESH)

    for i in range(NX):
        greet((lax.rem(c + 1, 8), i * NZ + edge_owner(i, c + 1, 0)))
        greet((lax.rem(c + 7, 8), i * NZ + edge_owner(i, c + 1, 1)))
    for off in PEERS:
        greet(peer(off))

    copies = []
    for t in range(2):
        for k in range(NCH):
            copies.append(pltpu.make_async_copy(vis_hbm.at[:, k, t, :], vis.at[t, :, k, :], in_sem.at[2 * NCH * t + k]))
            copies.append(pltpu.make_async_copy(model_hbm.at[:, k, t, :], model.at[t, :, k, :], in_sem.at[2 * NCH * t + NCH + k]))
    for copy in copies:
        copy.start()

    low = lax.broadcasted_iota(jnp.int32, (256, LANES), 0).astype(F32).astype(BF16)
    one, nil = jnp.ones((256, LANES), BF16), jnp.zeros((256, LANES), BF16)
    across = lax.broadcasted_iota(jnp.int32, (LANES, 256), 1).astype(F32).astype(BF16)
    one_t, nil_t = jnp.ones((LANES, 256), BF16), jnp.zeros((LANES, 256), BF16)

    def tables(g, _):
        src = pl.ds(pl.multiple_of(g * LANES, LANES), LANES)
        for side in range(2):
            per = W // LANES
            dst = pl.ds(pl.multiple_of((2 * (g // per) + side) * W + g % per * LANES, LANES), LANES)
            station = pairs[side : side + 1, src]
            row = (station & 255).astype(F32)
            rows = jnp.concatenate([jnp.broadcast_to(row, (16, LANES)).astype(BF16)] * 16, axis=0)
            table[:, dst] = jnp.where(rows == low, one, nil)
            column = jnp.broadcast_to(station.astype(F32), (LANES, LANES)).T
            for half in range(2):
                inside = (column - 256.0 * half).astype(BF16)
                inside = jnp.concatenate([inside] * 2, axis=1)
                table_t[dst, half * 256 : half * 256 + 256] = jnp.where(inside == across, one_t, nil_t)
        return 0

    lax.fori_loop(0, NB // LANES, tables, 0)

    for s in range(4):
        for k in range(8):
            gs[pl.ds(s * 64 + k, 8, stride=8), :] = init[k, :, s * LANES : (s + 1) * LANES]

    for copy in copies:
        copy.wait()

    def prepare(g, _):
        lanes = pl.ds(pl.multiple_of(g * LANES, LANES), LANES)
        v = [[vis[t, k, :, lanes] for k in range(8)] for t in range(2)]
        m = [[model[t, k, :, lanes] for k in range(8)] for t in range(2)]
        for_numer, for_denom = products(v, m)
        for n in range(16):
            numer[0, n, :, lanes] = for_numer[n][0]
            numer[1, n, :, lanes] = for_numer[n][1]
            denom[n, :, lanes] = for_denom[n]
        return 0

    lax.fori_loop(0, NB // LANES, prepare, 0)

    def iteration(step, _):
        for s in range(4):
            rows, lanes = (s // 2) * 128, slice((s % 2) * LANES, (s % 2 + 1) * LANES)
            for k in range(0, 8, 2):
                two = jnp.concatenate([gs[pl.ds(s * 64 + k + i, 8, stride=8), :] for i in range(2)], axis=0)
                high = two.astype(BF16)
                gains_lhs[rows + 8 * k : rows + 8 * k + 16, lanes] = high
                gains_lhs[rows + 64 + 8 * k : rows + 64 + 8 * k + 16, lanes] = (two - high.astype(F32)).astype(BF16)

        def lookup(i, side, gains):
            picked = jnp.dot(gains_lhs[...], table[:, (2 * i + side) * W : (2 * i + side + 1) * W], preferred_element_type=F32)
            for g in range(W // LANES):
                lanes = slice(i * W + g * LANES, i * W + (g + 1) * LANES)
                at = slice(g * LANES, (g + 1) * LANES)
                upper = jnp.broadcast_to(pairs[side : side + 1, lanes], (128, LANES)) >= 256
                chosen = jnp.where(upper, picked[128:, at], picked[:128, at])
                gains[:, side * W + g * LANES : side * W + (g + 1) * LANES] = chosen[:64] + chosen[64:]

        def compute(i, side, g, gains, terms):
            lanes = slice(i * W + g * LANES, i * W + (g + 1) * LANES)
            here = slice(side * W + g * LANES, side * W + (g + 1) * LANES)
            other = slice((1 - side) * W + g * LANES, (1 - side) * W + (g + 1) * LANES)
            gain = mat([gains[8 * k : 8 * k + 8, other] for k in range(8)])

            def pick(i, j, l, k):
                n = 8 * i + 4 * j + 2 * l + k
                return numer[0, n, :, lanes], numer[1, n, :, lanes]

            term = side_terms(side, pick, lambda n: denom[n, :, lanes], gain)
            for k in range(0, 12, 2):
                two = jnp.concatenate([term[k], term[k + 1]], axis=0)
                high = two.astype(BF16)
                terms[8 * k : 8 * k + 16, here] = high
                terms[96 + 8 * k : 112 + 8 * k, here] = (two - high.astype(F32)).astype(BF16)

        def collect(i, half):
            columns = pl.ds(pl.multiple_of(half * 256, 256), 256)
            return jnp.dot(terms[i][...], table_t[2 * i * W : 2 * (i + 1) * W, columns], preferred_element_type=F32)

        def collect_far(i):
            if i == 0:
                acc[...] = collect(i, far_half)
            else:
                acc[...] += collect(i, far_half)

        def stage(sums, half, at):
            for s in range(2):
                lanes = slice(s * LANES, (s + 1) * LANES)
                acc4[at + s] = sums[:96, lanes] + sums[96:, lanes]
                for k in range(NCH):
                    sb[step, 2 * half + s, k] = acc4[at + s, pl.ds(k, 12, stride=8), :]

        far_half = 1 - x // 2
        gains, terms = (gains0, gains1), (terms0, terms1, terms2, terms3)
        for side in range(2):
            lookup(0, side, gains0)
        for i in range(CHUNKS):
            matrix = []
            if i + 1 < CHUNKS:
                matrix += [functools.partial(lookup, i + 1, side, gains[(i + 1) % 2]) for side in range(2)]
            if i > 0:
                matrix.append(functools.partial(collect_far, i - 1))
            vector = [(side, g) for g in range(W // LANES) for side in range(2)]
            share = -(-len(vector) // len(matrix))
            for n, part in enumerate(matrix):
                part()
                for side, g in vector[n * share : (n + 1) * share]:
                    compute(i, side, g, gains[i % 2], terms[i])
        stage(acc[...] + collect(CHUNKS - 1, far_half), far_half, 0)

        @pl.when(step == 0)
        def _():
            edge = jnp.where((my_ch == 0) | (my_ch == NCH - 1), 32, 0)
            pl.semaphore_wait(barrier, 31 + edge)

        def send_sums(dx, dz):
            device = peer((dx, dz))
            tx, tz = device[1] // NZ, device[1] % NZ
            pltpu.make_async_remote_copy(
                src_ref=sb.at[step, tx, owned(tx, tz, c)],
                dst_ref=rb.at[step, b],
                send_sem=rs_send.at[step],
                recv_sem=rs_recv.at[step],
                device_id=device,
                device_id_type=MESH,
            ).start()

        to_far, to_near = 3 - 2 * (x % 2), 1 + 2 * (x % 2)
        for count in range(6, 0, -1):
            for dz in range(NZ):
                if hops((2, dz)) == count:
                    send_sums(2, dz)
                if hops((1, dz)) == count:
                    send_sums(to_far, dz)
        near_half = 1 - far_half
        stage(functools.reduce(jnp.add, [collect(i, near_half) for i in range(CHUNKS)]), near_half, 2)
        for count in range(5, 0, -1):
            for dz in range(NZ):
                if hops((1, dz)) == count:
                    send_sums(to_near, dz)
                if hops((0, dz)) == count:
                    send_sums(0, dz)
        rb[step, b] = sb[step, x, my_ch]
        landed = rb.at[step, pl.ds(0, 31)]
        pltpu.make_async_copy(landed, landed, rs_recv.at[step]).wait()

        total = rb[step, 0]
        for i in range(1, 32):
            total = total + rb[step, i]
        row = [total[k : k + 1, :] for k in range(12)]
        num = mat(row[:8])
        upper, lower = row[8] + RIDGE, row[9] + RIDGE
        off_real, off_imag = row[10], row[11]
        inv = 1.0 / (upper * lower - off_real * off_real - off_imag * off_imag)
        zero = jnp.zeros_like(upper)
        inverse = [
            [(lower * inv, zero), (-off_real * inv, -off_imag * inv)],
            [(-off_real * inv, off_imag * inv), (upper * inv, zero)],
        ]
        old = gs[pl.ds(pl.multiple_of(x * 64 + my_ch * 8, 8), 8), :]
        solved = jnp.concatenate(flat(mm(num, inverse)), axis=0)
        mine[step] = 0.5 * (solved + old)
        slot = x * 10 + my_ch + 1
        gb[step, slot] = mine[step]

        def give(device, there):
            pltpu.make_async_remote_copy(
                src_ref=mine.at[step],
                dst_ref=gb.at[step, there],
                send_sem=ag_send.at[step],
                recv_sem=ag_recv.at[step],
                device_id=device,
                device_id_type=MESH,
            ).start()

        for ch, dc, there in ((0, -1, x * 10 + 9), (NCH - 1, 1, x * 10)):

            @pl.when(my_ch == ch)
            def _():
                for far in range(7, -1, -1):
                    for off in OFFSETS:
                        if hops(off) + 1 == far:
                            give(peer(off, dc), there)
                        if hops(off) == far and far > 0:
                            give(peer(off), slot)

        @pl.when((my_ch > 0) & (my_ch < NCH - 1))
        def _():
            for off in PEERS:
                give(peer(off), slot)

        landed = gb.at[step, pl.ds(0, 39)]
        pltpu.make_async_copy(landed, landed, ag_recv.at[step]).wait()

        for s in range(4):
            edge_before = jnp.where(c == 0, 0.0, gb[step, s * 10])
            edge_after = jnp.where(c == 7, 0.0, gb[step, s * 10 + 9])
            near = [edge_before] + [gb[step, s * 10 + k] for k in range(1, 9)] + [edge_after]
            for k in range(NCH):
                total = near[k] + 2.0 * near[k + 1] + near[k + 2]
                weight = 0.25
                if k == 0:
                    weight = jnp.where(c == 0, 1.0 / 3.0, 0.25)
                if k == NCH - 1:
                    weight = jnp.where(c == 7, 1.0 / 3.0, 0.25)
                gs[s * 64 + 8 * k : s * 64 + 8 * k + 8, :] = total * weight

        gone = rb.at[step, pl.ds(0, 31)]
        pltpu.make_async_copy(gone, gone, rs_send.at[step]).wait()
        gone = gb.at[step, pl.ds(0, 31)]
        pltpu.make_async_copy(gone, gone, ag_send.at[step]).wait()

        @pl.when((my_ch == 0) | (my_ch == NCH - 1))
        def _():
            gone = gb.at[step, pl.ds(0, 32)]
            pltpu.make_async_copy(gone, gone, ag_send.at[step]).wait()

        return 0

    lax.fori_loop(0, ITERS, iteration, 0)
    for s in range(4):
        for k in range(8):
            out[k, :, s * LANES : (s + 1) * LANES] = gs[pl.ds(s * 64 + k, 8, stride=8), :]


def body(visibility, model_vis, station_pairs, init_gains):
    vmem = pl.BlockSpec(memory_space=pltpu.VMEM)
    hbm = pl.BlockSpec(memory_space=pl.ANY)
    return pl.pallas_call(
        kernel,
        out_shape=jax.ShapeDtypeStruct((8, NCH, NS), F32),
        in_specs=[hbm, hbm, vmem, vmem],
        out_specs=vmem,
        scratch_shapes=[
            pltpu.VMEM((2, 8, NCH, NB), F32),
            pltpu.VMEM((2, 8, NCH, NB), F32),
            pltpu.VMEM((2, 16, NCH, NB), F32),
            pltpu.VMEM((16, NCH, NB), F32),
            pltpu.VMEM((256, 2 * NB), BF16),
            pltpu.VMEM((2 * NB, NS), BF16),
            pltpu.VMEM((256, 256), BF16),
            pltpu.VMEM((64, 2 * W), F32),
            pltpu.VMEM((64, 2 * W), F32),
            pltpu.VMEM((192, 2 * W), BF16),
            pltpu.VMEM((192, 2 * W), BF16),
            pltpu.VMEM((192, 2 * W), BF16),
            pltpu.VMEM((192, 2 * W), BF16),
            pltpu.VMEM((192, 256), F32),
            pltpu.VMEM((4, 96, LANES), F32),
            pltpu.VMEM((256, LANES), F32),
            pltpu.VMEM((ITERS, 4, NCH, 12, LANES), F32),
            pltpu.VMEM((ITERS, 32, 12, LANES), F32),
            pltpu.VMEM((ITERS, 40, 8, LANES), F32),
            pltpu.VMEM((ITERS, 8, LANES), F32),
            pltpu.SemaphoreType.DMA((32,)),
            pltpu.SemaphoreType.DMA((ITERS,)),
            pltpu.SemaphoreType.DMA((ITERS,)),
            pltpu.SemaphoreType.DMA((ITERS,)),
            pltpu.SemaphoreType.DMA((ITERS,)),
        ],
        compiler_params=pltpu.CompilerParams(collective_id=0, has_side_effects=True, vmem_limit_bytes=56 << 20),
    )(visibility, model_vis, station_pairs, init_gains)


def solution(mesh):
    in_specs = (
        P(None, "chan", None, "bl"),
        P(None, "chan", None, "bl"),
        P(None, "bl"),
        P(None, "chan", None),
    )
    return jax.shard_map(body, mesh=mesh, in_specs=in_specs, out_specs=P(None, "chan", None), check_vma=False)
```

```python
import functools

import jax
import jax.numpy as jnp
from jax import lax
from jax.experimental import pallas as pl
from jax.experimental.pallas import tpu as pltpu
from jax.sharding import PartitionSpec as P

ITERS = 3
RIDGE = 1.0
NX, NZ, NCH = 4, 8, 8
NS, NB = 512, 4096
LANES = 128
W = 1024
CHUNKS = NB // W
MESH = pl.DeviceIdType.MESH
F32, BF16 = jnp.float32, jnp.bfloat16


def hops(off):
    return min(off[0], NX - off[0]) + min(off[1], NZ - off[1])


OFFSETS = sorted([(i, j) for i in range(NX) for j in range(NZ)], key=lambda o: -hops(o))
PEERS = [o for o in OFFSETS if o != (0, 0)]


def cmul(a, b, ca=False, cb=False):
    (ar, ai), (br, bi) = a, b
    re = ar * br + ai * bi if ca != cb else ar * br - ai * bi
    if ca:
        im = ar * bi - ai * br if not cb else -(ar * bi + ai * br)
    else:
        im = ai * br - ar * bi if cb else ar * bi + ai * br
    return re, im


def cadd(a, b):
    return a[0] + b[0], a[1] + b[1]


def mm(a, b, ah=False, bh=False):
    def one(i, j):
        parts = []
        for k in range(2):
            left = a[k][i] if ah else a[i][k]
            right = b[j][k] if bh else b[k][j]
            parts.append(cmul(left, right, ah, bh))
        return cadd(*parts)

    return [[one(i, j) for j in range(2)] for i in range(2)]


def square(z):
    return z[0] * z[0] + z[1] * z[1]


def tree(terms):
    while len(terms) > 1:
        terms = [terms[i] + terms[i + 1] for i in range(0, len(terms), 2)]
    return terms[0]


def mat(v):
    return [[(v[2 * i + j], v[4 + 2 * i + j]) for j in range(2)] for i in range(2)]


def flat(m):
    return [m[i][j][p] for p in range(2) for i in range(2) for j in range(2)]


def over_time(one):
    return cadd(one(0), one(1))


def products(vis, model):
    v, m = [mat(a) for a in vis], [mat(a) for a in model]
    numer = [
        over_time(lambda t: cmul(v[t][i][j], m[t][l][k], cb=True))
        for i in range(2) for j in range(2) for l in range(2) for k in range(2)
    ]

    def cross(a, b):
        return over_time(lambda t: cmul(m[t][a[0]][a[1]], m[t][b[0]][b[1]], cb=True))

    power = [square(m[0][i][j]) + square(m[1][i][j]) for i in range(2) for j in range(2)]
    u, w = cross((0, 0), (1, 1)), cross((0, 1), (1, 0))
    pairs = [cross((0, 0), (0, 1)), cross((1, 0), (1, 1)), cross((0, 0), (1, 0)), cross((0, 1), (1, 1))]
    mixed = [u[0] + w[0], w[1] - u[1], u[1] + w[1], u[0] - w[0]]
    return numer, power + [part for pair in pairs for part in pair] + mixed


def side_terms(side, numer, denom, gain):
    rows = []
    for i in range(2):
        for l in range(2):
            re, im = [], []
            for j in range(2):
                for k in range(2):
                    cr, ci = numer(i, j, l, k) if side == 0 else numer(j, i, k, l)
                    gr, gi = gain[j][k]
                    if side == 0:
                        re.append(cr * gr - ci * gi)
                        im.append(cr * gi + ci * gr)
                    else:
                        re.append(cr * gr + ci * gi)
                        im.append(cr * gi - ci * gr)
            rows.append((tree(re), tree(im)))
    out = [r[0] for r in rows] + [r[1] for r in rows]
    h00, h11 = square(gain[0][0]) + square(gain[1][0]), square(gain[0][1]) + square(gain[1][1])
    hr, hi = cadd(cmul(gain[0][0], gain[0][1], ca=True), cmul(gain[1][0], gain[1][1], ca=True))
    h2r, h2i = hr + hr, hi + hi
    d = [denom(n) for n in range(16)]
    if side == 0:
        out.append((d[0] * h00 + d[1] * h11) + (d[4] * h2r - d[5] * h2i))
        out.append((d[2] * h00 + d[3] * h11) + (d[6] * h2r - d[7] * h2i))
        out.append((d[8] * h00 + d[10] * h11) + (d[12] * hr + d[13] * hi))
        out.append((d[9] * h00 + d[11] * h11) + (d[14] * hr + d[15] * hi))
    else:
        out.append((d[0] * h00 + d[2] * h11) + (d[8] * h2r + d[9] * h2i))
        out.append((d[1] * h00 + d[3] * h11) + (d[10] * h2r + d[11] * h2i))
        out.append((d[4] * h00 + d[6] * h11) + (d[12] * hr + d[14] * hi))
        out.append((d[13] * hr + d[15] * hi) - (d[5] * h00 + d[7] * h11))
    return out


def kernel(vis_hbm, model_hbm, pairs, init, out, vis, model, numer, denom, table, table_t, gains_lhs, gains0, gains1, terms0, terms1, terms2, terms3, acc, acc4, gs, sb, rb, gb, mine, in_sem, rs_send, rs_recv, ag_send, ag_recv):
    c, b = lax.axis_index("chan"), lax.axis_index("bl")
    x, z = b // NZ, b % NZ
    def owned(x, z, c):
        place = lax.rem(z + x + 2 * (c % 2), NCH)
        return jnp.where(place < 4, place, jnp.where(place == 4, NCH - 1, place - 1))

    def edge_owner(x, c, last):
        return lax.rem(16 + 4 * last - x - 2 * (c % 2), NZ)

    my_ch = owned(x, z, c)

    def peer(off, dc=0):
        dx, dz = off
        return (lax.rem(c + dc + 8, 8), lax.rem(x + dx, NX) * NZ + lax.rem(z + dz, NZ))

    barrier = pltpu.get_barrier_semaphore()

    def greet(device):
        pl.semaphore_signal(barrier, inc=1, device_id=device, device_id_type=MESH)

    for i in range(NX):
        greet((lax.rem(c + 1, 8), i * NZ + edge_owner(i, c + 1, 0)))
        greet((lax.rem(c + 7, 8), i * NZ + edge_owner(i, c + 1, 1)))
    for off in PEERS:
        greet(peer(off))

    copies = []
    for t in range(2):
        for k in range(NCH):
            copies.append(pltpu.make_async_copy(vis_hbm.at[:, k, t, :], vis.at[t, :, k, :], in_sem.at[2 * NCH * t + k]))
            copies.append(pltpu.make_async_copy(model_hbm.at[:, k, t, :], model.at[t, :, k, :], in_sem.at[2 * NCH * t + NCH + k]))
    for copy in copies:
        copy.start()

    low = lax.broadcasted_iota(jnp.int32, (256, LANES), 0).astype(F32).astype(BF16)
    one, nil = jnp.ones((256, LANES), BF16), jnp.zeros((256, LANES), BF16)
    across = lax.broadcasted_iota(jnp.int32, (LANES, 256), 1).astype(F32).astype(BF16)
    one_t, nil_t = jnp.ones((LANES, 256), BF16), jnp.zeros((LANES, 256), BF16)

    def tables(g, _):
        src = pl.ds(pl.multiple_of(g * LANES, LANES), LANES)
        for side in range(2):
            per = W // LANES
            dst = pl.ds(pl.multiple_of((2 * (g // per) + side) * W + g % per * LANES, LANES), LANES)
            station = pairs[side : side + 1, src]
            row = (station & 255).astype(F32)
            rows = jnp.concatenate([jnp.broadcast_to(row, (16, LANES)).astype(BF16)] * 16, axis=0)
            table[:, dst] = jnp.where(rows == low, one, nil)
            column = jnp.broadcast_to(station.astype(F32), (LANES, LANES)).T
            for half in range(2):
                inside = (column - 256.0 * half).astype(BF16)
                inside = jnp.concatenate([inside] * 2, axis=1)
                table_t[dst, half * 256 : half * 256 + 256] = jnp.where(inside == across, one_t, nil_t)
        return 0

    lax.fori_loop(0, NB // LANES, tables, 0, unroll=2)

    for s in range(4):
        for k in range(8):
            gs[pl.ds(s * 64 + k, 8, stride=8), :] = init[k, :, s * LANES : (s + 1) * LANES]

    for copy in copies:
        copy.wait()

    def prepare(g, _):
        lanes = pl.ds(pl.multiple_of(g * LANES, LANES), LANES)
        v = [[vis[t, k, :, lanes] for k in range(8)] for t in range(2)]
        m = [[model[t, k, :, lanes] for k in range(8)] for t in range(2)]
        for_numer, for_denom = products(v, m)
        for n in range(16):
            numer[0, n, :, lanes] = for_numer[n][0]
            numer[1, n, :, lanes] = for_numer[n][1]
            denom[n, :, lanes] = for_denom[n]
        return 0

    lax.fori_loop(0, NB // LANES, prepare, 0)

    def iteration(step, _):
        for s in range(4):
            rows, lanes = (s // 2) * 128, slice((s % 2) * LANES, (s % 2 + 1) * LANES)
            for k in range(0, 8, 2):
                two = jnp.concatenate([gs[pl.ds(s * 64 + k + i, 8, stride=8), :] for i in range(2)], axis=0)
                high = two.astype(BF16)
                gains_lhs[rows + 8 * k : rows + 8 * k + 16, lanes] = high
                gains_lhs[rows + 64 + 8 * k : rows + 64 + 8 * k + 16, lanes] = (two - high.astype(F32)).astype(BF16)

        def lookup(i, side, gains):
            picked = jnp.dot(gains_lhs[...], table[:, (2 * i + side) * W : (2 * i + side + 1) * W], preferred_element_type=F32)
            for g in range(W // LANES):
                lanes = slice(i * W + g * LANES, i * W + (g + 1) * LANES)
                at = slice(g * LANES, (g + 1) * LANES)
                upper = jnp.broadcast_to(pairs[side : side + 1, lanes], (128, LANES)) >= 256
                chosen = jnp.where(upper, picked[128:, at], picked[:128, at])
                gains[:, side * W + g * LANES : side * W + (g + 1) * LANES] = chosen[:64] + chosen[64:]

        def compute(i, side, g, gains, terms):
            lanes = slice(i * W + g * LANES, i * W + (g + 1) * LANES)
            here = slice(side * W + g * LANES, side * W + (g + 1) * LANES)
            other = slice((1 - side) * W + g * LANES, (1 - side) * W + (g + 1) * LANES)
            gain = mat([gains[8 * k : 8 * k + 8, other] for k in range(8)])

            def pick(i, j, l, k):
                n = 8 * i + 4 * j + 2 * l + k
                return numer[0, n, :, lanes], numer[1, n, :, lanes]

            term = side_terms(side, pick, lambda n: denom[n, :, lanes], gain)
            for k in range(0, 12, 2):
                two = jnp.concatenate([term[k], term[k + 1]], axis=0)
                high = two.astype(BF16)
                terms[8 * k : 8 * k + 16, here] = high
                terms[96 + 8 * k : 112 + 8 * k, here] = (two - high.astype(F32)).astype(BF16)

        def collect(i, half):
            columns = pl.ds(pl.multiple_of(half * 256, 256), 256)
            return jnp.dot(terms[i][...], table_t[2 * i * W : 2 * (i + 1) * W, columns], preferred_element_type=F32)

        def collect_far(i):
            if i == 0:
                acc[...] = collect(i, far_half)
            else:
                acc[...] += collect(i, far_half)

        def stage(sums, half, at):
            for s in range(2):
                lanes = slice(s * LANES, (s + 1) * LANES)
                acc4[at + s] = sums[:96, lanes] + sums[96:, lanes]
                for k in range(NCH):
                    sb[step, 2 * half + s, k] = acc4[at + s, pl.ds(k, 12, stride=8), :]

        far_half = 1 - x // 2
        gains, terms = (gains0, gains1), (terms0, terms1, terms2, terms3)
        for side in range(2):
            lookup(0, side, gains0)
        for i in range(CHUNKS):
            matrix = []
            if i + 1 < CHUNKS:
                matrix += [functools.partial(lookup, i + 1, side, gains[(i + 1) % 2]) for side in range(2)]
            if i > 0:
                matrix.append(functools.partial(collect_far, i - 1))
            vector = [(side, g) for g in range(W // LANES) for side in range(2)]
            share = -(-len(vector) // len(matrix))
            for n, part in enumerate(matrix):
                part()
                for side, g in vector[n * share : (n + 1) * share]:
                    compute(i, side, g, gains[i % 2], terms[i])
        stage(acc[...] + collect(CHUNKS - 1, far_half), far_half, 0)

        @pl.when(step == 0)
        def _():
            edge = jnp.where((my_ch == 0) | (my_ch == NCH - 1), 32, 0)
            pl.semaphore_wait(barrier, 31 + edge)

        def send_sums(dx, dz):
            device = peer((dx, dz))
            tx, tz = device[1] // NZ, device[1] % NZ
            pltpu.make_async_remote_copy(
                src_ref=sb.at[step, tx, owned(tx, tz, c)],
                dst_ref=rb.at[step, b],
                send_sem=rs_send.at[step],
                recv_sem=rs_recv.at[step],
                device_id=device,
                device_id_type=MESH,
            ).start()

        to_far, to_near = 3 - 2 * (x % 2), 1 + 2 * (x % 2)
        for count in range(6, 0, -1):
            for dz in range(NZ):
                if hops((2, dz)) == count:
                    send_sums(2, dz)
                if hops((1, dz)) == count:
                    send_sums(to_far, dz)
        near_half = 1 - far_half
        stage(functools.reduce(jnp.add, [collect(i, near_half) for i in range(CHUNKS)]), near_half, 2)
        for count in range(5, 0, -1):
            for dz in range(NZ):
                if hops((1, dz)) == count:
                    send_sums(to_near, dz)
                if hops((0, dz)) == count:
                    send_sums(0, dz)
        rb[step, b] = sb[step, x, my_ch]
        landed = rb.at[step, pl.ds(0, 31)]
        pltpu.make_async_copy(landed, landed, rs_recv.at[step]).wait()

        total = rb[step, 0]
        for i in range(1, 32):
            total = total + rb[step, i]
        row = [total[k : k + 1, :] for k in range(12)]
        num = mat(row[:8])
        upper, lower = row[8] + RIDGE, row[9] + RIDGE
        off_real, off_imag = row[10], row[11]
        inv = 1.0 / (upper * lower - off_real * off_real - off_imag * off_imag)
        zero = jnp.zeros_like(upper)
        inverse = [
            [(lower * inv, zero), (-off_real * inv, -off_imag * inv)],
            [(-off_real * inv, off_imag * inv), (upper * inv, zero)],
        ]
        old = gs[pl.ds(pl.multiple_of(x * 64 + my_ch * 8, 8), 8), :]
        solved = jnp.concatenate(flat(mm(num, inverse)), axis=0)
        mine[step] = 0.5 * (solved + old)
        slot = x * 10 + my_ch + 1
        gb[step, slot] = mine[step]

        def give(device, there):
            pltpu.make_async_remote_copy(
                src_ref=mine.at[step],
                dst_ref=gb.at[step, there],
                send_sem=ag_send.at[step],
                recv_sem=ag_recv.at[step],
                device_id=device,
                device_id_type=MESH,
            ).start()

        for ch, dc, there in ((0, -1, x * 10 + 9), (NCH - 1, 1, x * 10)):

            @pl.when(my_ch == ch)
            def _():
                for far in range(7, -1, -1):
                    for off in OFFSETS:
                        if hops(off) + 1 == far:
                            give(peer(off, dc), there)
                        if hops(off) == far and far > 0:
                            give(peer(off), slot)

        @pl.when((my_ch > 0) & (my_ch < NCH - 1))
        def _():
            for off in PEERS:
                give(peer(off), slot)

        landed = gb.at[step, pl.ds(0, 39)]
        pltpu.make_async_copy(landed, landed, ag_recv.at[step]).wait()

        for s in range(4):
            edge_before = jnp.where(c == 0, 0.0, gb[step, s * 10])
            edge_after = jnp.where(c == 7, 0.0, gb[step, s * 10 + 9])
            near = [edge_before] + [gb[step, s * 10 + k] for k in range(1, 9)] + [edge_after]
            for k in range(NCH):
                total = near[k] + 2.0 * near[k + 1] + near[k + 2]
                weight = 0.25
                if k == 0:
                    weight = jnp.where(c == 0, 1.0 / 3.0, 0.25)
                if k == NCH - 1:
                    weight = jnp.where(c == 7, 1.0 / 3.0, 0.25)
                gs[s * 64 + 8 * k : s * 64 + 8 * k + 8, :] = total * weight

        gone = rb.at[step, pl.ds(0, 31)]
        pltpu.make_async_copy(gone, gone, rs_send.at[step]).wait()
        gone = gb.at[step, pl.ds(0, 31)]
        pltpu.make_async_copy(gone, gone, ag_send.at[step]).wait()

        @pl.when((my_ch == 0) | (my_ch == NCH - 1))
        def _():
            gone = gb.at[step, pl.ds(0, 32)]
            pltpu.make_async_copy(gone, gone, ag_send.at[step]).wait()

        return 0

    lax.fori_loop(0, ITERS, iteration, 0)
    for s in range(4):
        for k in range(8):
            out[k, :, s * LANES : (s + 1) * LANES] = gs[pl.ds(s * 64 + k, 8, stride=8), :]


def body(visibility, model_vis, station_pairs, init_gains):
    vmem = pl.BlockSpec(memory_space=pltpu.VMEM)
    hbm = pl.BlockSpec(memory_space=pl.ANY)
    return pl.pallas_call(
        kernel,
        out_shape=jax.ShapeDtypeStruct((8, NCH, NS), F32),
        in_specs=[hbm, hbm, vmem, vmem],
        out_specs=vmem,
        scratch_shapes=[
            pltpu.VMEM((2, 8, NCH, NB), F32),
            pltpu.VMEM((2, 8, NCH, NB), F32),
            pltpu.VMEM((2, 16, NCH, NB), F32),
            pltpu.VMEM((16, NCH, NB), F32),
            pltpu.VMEM((256, 2 * NB), BF16),
            pltpu.VMEM((2 * NB, NS), BF16),
            pltpu.VMEM((256, 256), BF16),
            pltpu.VMEM((64, 2 * W), F32),
            pltpu.VMEM((64, 2 * W), F32),
            pltpu.VMEM((192, 2 * W), BF16),
            pltpu.VMEM((192, 2 * W), BF16),
            pltpu.VMEM((192, 2 * W), BF16),
            pltpu.VMEM((192, 2 * W), BF16),
            pltpu.VMEM((192, 256), F32),
            pltpu.VMEM((4, 96, LANES), F32),
            pltpu.VMEM((256, LANES), F32),
            pltpu.VMEM((ITERS, 4, NCH, 12, LANES), F32),
            pltpu.VMEM((ITERS, 32, 12, LANES), F32),
            pltpu.VMEM((ITERS, 40, 8, LANES), F32),
            pltpu.VMEM((ITERS, 8, LANES), F32),
            pltpu.SemaphoreType.DMA((32,)),
            pltpu.SemaphoreType.DMA((ITERS,)),
            pltpu.SemaphoreType.DMA((ITERS,)),
            pltpu.SemaphoreType.DMA((ITERS,)),
            pltpu.SemaphoreType.DMA((ITERS,)),
        ],
        compiler_params=pltpu.CompilerParams(collective_id=0, has_side_effects=True, vmem_limit_bytes=56 << 20),
    )(visibility, model_vis, station_pairs, init_gains)


def solution(mesh):
    in_specs = (
        P(None, "chan", None, "bl"),
        P(None, "chan", None, "bl"),
        P(None, "bl"),
        P(None, "chan", None),
    )
    return jax.shard_map(body, mesh=mesh, in_specs=in_specs, out_specs=P(None, "chan", None), check_vma=False)
```
